256 devices in a mesh: region: 4 (over y), dom: 64 (over x, z, core).
Axes of the slice: x: 4, y: 4, z: 8, core: 2. Of those that a mesh axis runs over, the one named last changes fastest.
Arguments:
- features: bfloat16 [65536, 768], P(('region', 'dom')), may hold values from -6 to 6
- cotangent: bfloat16 [65536, 768], P(('region', 'dom')), may hold values from -6 to 6
- conv_weight: bfloat16 [2, 64, 128], replicated, may hold values from -0.5 to 0.5
- conv_bias: float32 [128], replicated, may hold values from -3 to 3
- diff_weight: bfloat16 [3, 64, 64], replicated, may hold values from -0.75 to 0.75
- edge_tiles: bfloat16 [3072, 128, 128], P(('region', 'dom')), may hold values from -0.21875 to 0.21875
- tile_source: int32 [256, 12], P(('region', 'dom')), may hold values from 0 to 9, as said below
- tile_target: int32 [256, 12], P(('region', 'dom')), may hold values from 0 to 1
- tile_count: int32 [256], P(('region', 'dom')), may hold values from 5 to 12, as said below
Outputs:
- mixed: bfloat16 [65536, 768], P(('region', 'dom'))
- grad_features: bfloat16 [65536, 768], P(('region', 'dom'))
- grad_diff: float32 [3, 64, 64], replicated
- grad_conv: float32 [2, 64, 128], replicated
- grad_bias: float32 [128], replicated
The draws below stay inside these ranges and needn't reach their ends.
Inputs may be any that keep to these rules, and one draw needn't show every extreme that they name: `tile_source`: s // 2 chooses the device itself, its lower or upper neighbour along dom, or its lower or upper neighbour along region; s % 2 is a block of that device; the first five slots of each device name five different choices of neighbour. `tile_count`: slots at or past the count are not part of the graph; some devices use all 12 slots.
All inputs are finite; a program needn't handle non-finite values.
Results may differ from the reference program's by a relative error of at most 0.0055.
Values may be sent and summed in bfloat16 or wider, within the bound.
No kernel may reach another device: no remote copies, remote signals or barrier semaphores. Data moves between devices by JAX's collectives and lax.ppermute only.
A program may use at most 128 MiB of HBM per device.

```python
import math
import jax
import jax.numpy as jnp
from jax import lax

C = 64
STEPS = 12
BLK = 128
NB_DEV = 2
TILES_PER_BLOCK = 6
TILE_SLOTS = 12
CELLS = 65536
N_REGION = 4
N_DOM = 64
DEVICES = 256


def draw_tile_count(key, part):
    key = jax.random.fold_in(key, 5)
    keys = jax.random.split(key, 4)
    lightest = max(5, TILE_SLOTS // 4)
    middle = max(lightest, TILE_SLOTS // 2)
    common = jax.random.randint(keys[0], (DEVICES,), lightest, middle + 1)
    busiest = jax.random.randint(keys[1], (DEVICES,), 0, 8) == 0
    first_full = jax.random.randint(keys[2], (), 0, DEVICES)
    first_light = (first_full + 1 + jax.random.randint(keys[3], (), 0, DEVICES - 1)) % DEVICES
    places = jnp.arange(DEVICES)
    counts = jnp.where(busiest | (places == first_full), TILE_SLOTS, common)
    counts = jnp.where(places == first_light, lightest, counts)
    return counts.astype(jnp.int32)


def draw_tile_source(key, part):
    key = jax.random.fold_in(key, 7)
    keys = jax.random.split(key, 3)
    offsets = jax.random.randint(keys[0], (DEVICES, 1), 0, 5)
    slots = jnp.arange(TILE_SLOTS, dtype=jnp.int32)[None, :]
    free_way = jax.random.randint(keys[1], (DEVICES, TILE_SLOTS), 0, 5)
    direction = jnp.where(slots < 5, (slots + offsets) % 5, free_way)
    inside = jax.random.randint(keys[2], (DEVICES, TILE_SLOTS), 0, NB_DEV)
    return (direction * NB_DEV + inside).astype(jnp.int32)


def set_ends(drawn, rng, smallest, top_value):
    extent = drawn.shape
    place = [jax.random.randint(jax.random.fold_in(rng, axis), (), 0, extent[axis]) for axis in range(len(extent))]
    drawn = drawn.at[tuple(place)].set(smallest)
    longest = extent.index(max(extent))
    place[longest] = (place[longest] + 1) % extent[longest]
    return drawn.at[tuple(place)].set(top_value)


def levels(key, extent, cuts, smallest, top_value):
    level = 1.0
    for position, parts in cuts:
        heights = jax.random.uniform(jax.random.fold_in(jax.random.fold_in(key, 6), position), (parts,), jnp.float32, smallest / len(cuts), top_value / len(cuts))
        level = level * jnp.repeat(jnp.exp(heights), extent[position] // parts).reshape((-1,) + (1,) * (len(extent) - 1 - position))
    return level


def noise(stream_key, shape, spread, reach, pieces=(), kind=jnp.bfloat16):
    factor_of = levels(stream_key, shape, pieces, -0.22, 0.18) if pieces else 1.0
    values = jax.random.normal(stream_key, shape, jnp.float32) * spread * factor_of
    return jnp.minimum(jnp.maximum(values, -reach), reach).astype(kind)


def setup_inputs(seed: int = 0) -> dict:
    key_list = jax.random.split(jax.random.key(seed), 10)
    features = noise(key_list[0], (CELLS, STEPS * C), 1.0, 6.0, ((0, 256),))
    cotangent = noise(key_list[1], (CELLS, STEPS * C), 1.0, 6.0, ((0, 256),))
    conv_weight = noise(key_list[2], (2, C, 2 * C), (2 * C) ** -0.5, 0.5)
    conv_bias = noise(key_list[3], (2 * C,), 0.5, 3.0, (), jnp.float32)
    diff_weight = noise(key_list[4], (3, C, C), C ** -0.5, 0.75)
    edge_tiles = noise(key_list[5], (DEVICES * TILE_SLOTS, BLK, BLK), (BLK * TILES_PER_BLOCK) ** -0.5, 0.21875, ((0, 256),))
    tile_source = draw_tile_source(jax.random.fold_in(key_list[9], 71), 0)
    tile_target = set_ends(jax.random.randint(key_list[7], (DEVICES, TILE_SLOTS), 0, NB_DEV), jax.random.fold_in(key_list[7], 1), 0, NB_DEV - 1).astype(jnp.int32)
    tile_count = draw_tile_count(jax.random.fold_in(key_list[9], 71), 0)
    return {"features": features, "cotangent": cotangent, "conv_weight": conv_weight, "conv_bias": conv_bias, "diff_weight": diff_weight, "edge_tiles": edge_tiles, "tile_source": tile_source, "tile_target": tile_target, "tile_count": tile_count}


DOM_SHIFT = (0, -1, 1, 0, 0)
REGION_SHIFT = (0, 0, 0, -1, 1)

def source_block(device, source):
    neighbour = (source // NB_DEV).astype(jnp.int32)
    inside = (source % NB_DEV).astype(jnp.int32)
    region_at = device // N_DOM
    dom_at = device % N_DOM
    region_step = jnp.array(REGION_SHIFT, jnp.int32)[neighbour]
    dom_step = jnp.array(DOM_SHIFT, jnp.int32)[neighbour]
    region_from = (region_at + region_step) % N_REGION
    dom_from = (dom_at + dom_step) % N_DOM
    return ((region_from * N_DOM + dom_from) * NB_DEV + inside).astype(jnp.int32)

def diffuse(field, edge_tiles, tile_source, tile_target, tile_count, transpose):
    tile_table = edge_tiles.reshape(DEVICES, TILE_SLOTS, BLK, BLK)

    def per_device(device, totals):
        device = device.astype(jnp.int32)

        def per_tile(slot_index, inner):
            slot_index = slot_index.astype(jnp.int32)
            remote = source_block(device, tile_source[device, slot_index])
            own_block = (device * NB_DEV + tile_target[device, slot_index]).astype(jnp.int32)
            matrix = tile_table[device, slot_index]
            if transpose:
                matrix = matrix.T
                read_at, write_at = (own_block, remote)
            else:
                read_at, write_at = (remote, own_block)
            source_rows = lax.dynamic_index_in_dim(field, read_at, 0, keepdims=False)
            product = jnp.dot(matrix, source_rows, preferred_element_type=jnp.float32)
            return inner.at[write_at].add(product)
        return lax.fori_loop(jnp.int32(0), tile_count[device], per_tile, totals)
    start = jnp.zeros(field.shape, jnp.float32)
    return lax.fori_loop(jnp.int32(0), jnp.int32(DEVICES), per_device, start)

def channel_mix(left, right):
    return jnp.einsum('nti,io->nto', left.astype(jnp.float32), right.astype(jnp.float32))

def outer_sum(left, right):
    return jnp.einsum('nti,nto->io', left.astype(jnp.float32), right.astype(jnp.float32))

def reference(features, cotangent, conv_weight, conv_bias, diff_weight, edge_tiles, tile_source, tile_target, tile_count):
    block_total = CELLS // BLK

    def hop(field, transpose):
        blocked = field.reshape(block_total, BLK, STEPS * C)
        result = diffuse(blocked, edge_tiles, tile_source, tile_target, tile_count, transpose)
        return result.reshape(CELLS, STEPS, C)
    inputs = features.reshape(CELLS, STEPS, C)
    earlier = jnp.concatenate([jnp.zeros((CELLS, 1, C), inputs.dtype), inputs[:, :-1]], axis=1)
    pre = channel_mix(inputs, conv_weight[0]) + channel_mix(earlier, conv_weight[1]) + conv_bias
    filt = jnp.tanh(pre[..., :C])
    opened = jax.nn.sigmoid(pre[..., C:])
    gated = (filt * opened).astype(jnp.bfloat16)
    hop_one = hop(gated, False).astype(jnp.bfloat16)
    hop_two = hop(hop_one, False).astype(jnp.bfloat16)
    mixed = inputs.astype(jnp.float32) + channel_mix(gated, diff_weight[0]) + channel_mix(hop_one, diff_weight[1]) + channel_mix(hop_two, diff_weight[2])
    mixed = mixed.astype(jnp.bfloat16).reshape(CELLS, STEPS * C)
    upstream = cotangent.reshape(CELLS, STEPS, C)
    back_two = channel_mix(upstream, diff_weight[2].T).astype(jnp.bfloat16)
    back_one = (channel_mix(upstream, diff_weight[1].T) + hop(back_two, True)).astype(jnp.bfloat16)
    back_zero = channel_mix(upstream, diff_weight[0].T) + hop(back_one, True)
    back_filter = back_zero * opened * (1.0 - filt * filt)
    back_gate = back_zero * filt * opened * (1.0 - opened)
    back_pre = jnp.concatenate([back_filter, back_gate], axis=-1).astype(jnp.bfloat16)
    later = jnp.concatenate([back_pre[:, 1:], jnp.zeros((CELLS, 1, 2 * C), back_pre.dtype)], axis=1)
    grad_features = upstream.astype(jnp.float32) + channel_mix(back_pre, conv_weight[0].T) + channel_mix(later, conv_weight[1].T)
    grad_features = grad_features.astype(jnp.bfloat16).reshape(CELLS, STEPS * C)
    scale = 1.0 / math.sqrt(CELLS * STEPS)
    grad_diff = jnp.stack([outer_sum(gated, upstream), outer_sum(hop_one, upstream), outer_sum(hop_two, upstream)]) * scale
    grad_conv = jnp.stack([outer_sum(inputs, back_pre), outer_sum(earlier, back_pre)]) * scale
    grad_bias = lax.optimization_barrier(jnp.sum(back_pre.astype(jnp.float32), axis=(0, 1))) * scale
    return (mixed, grad_features, grad_diff, grad_conv, grad_bias)
```

```python
import math

import jax
import jax.numpy as jnp
from jax import lax
from jax.experimental import pallas as pl
from jax.experimental.pallas import tpu as pltpu
from jax.sharding import PartitionSpec as P

BF16 = jnp.bfloat16
F32 = jnp.float32
CH = 64
PAIR = 2 * CH
BLK = 128
ROWS = 256
DIFF_ROWS = 128
BIAS_ROW = 224

VMEM = pl.BlockSpec(memory_space=pltpu.VMEM)
SMEM = pl.BlockSpec(memory_space=pltpu.SMEM)


def shift(block, axis, distance):
    count = lax.axis_size(axis)
    return lax.ppermute(block, axis, [(i, (i + distance) % count) for i in range(count)])


def call(body, outs, args, specs, flops, scratch=()):
    moved = sum(a.size * a.dtype.itemsize for a in args)
    moved += sum(math.prod(s) * jnp.dtype(d).itemsize for s, d in outs)
    return pl.pallas_call(
        body,
        out_shape=[jax.ShapeDtypeStruct(s, d) for s, d in outs],
        in_specs=specs,
        out_specs=[VMEM] * len(outs),
        scratch_shapes=list(scratch),
        compiler_params=pltpu.CompilerParams(vmem_limit_bytes=40 * 1024 * 1024),
        cost_estimate=pl.CostEstimate(flops=flops, bytes_accessed=moved, transcendentals=0),
    )(*args)


def dot(a, b):
    return jnp.dot(a, b, preferred_element_type=F32)


def dot_nt(a, b):
    return lax.dot_general(a, b, (((1,), (1,)), ((), ())), preferred_element_type=F32)


def dot_tn(a, b):
    return lax.dot_general(a, b, (((0,), (0,)), ((), ())), preferred_element_type=F32)


def place(rows, cols, offset_of):
    r = lax.broadcasted_iota(jnp.int32, (rows, cols), 0)
    c = lax.broadcasted_iota(jnp.int32, (rows, cols), 1)
    return jnp.where(c == offset_of(r), 1.0, 0.0).astype(BF16)


def low_lanes(shape):
    return lax.broadcasted_iota(jnp.int32, shape, 1) < CH


def half_turn(v):
    return pltpu.roll(v, CH, 1)


def conv_table(w0, w1):
    even = place(PAIR, 2 * PAIR, lambda r: jnp.where(r < CH, r, r + CH))
    odd = place(PAIR, 2 * PAIR, lambda r: jnp.where(r < CH, r + CH, r + PAIR))
    tap1_even = dot(w1, even)
    tap0_even = dot(w0, even)
    tap1_odd = dot(w1, odd)
    tap0_odd = dot(w0, odd)
    rows = [jnp.zeros_like(tap1_even), tap1_even, tap0_even + tap1_odd, tap0_odd]
    return jnp.concatenate(rows, axis=0).astype(BF16)


def diff_table(w):
    low = place(CH, PAIR, lambda r: r)
    high = place(CH, PAIR, lambda r: r + CH)
    return jnp.concatenate([dot(w, low), dot(w, high)], axis=0).astype(BF16)


def pairs(ref, j):
    return ref[:, j * PAIR : (j + 1) * PAIR]


def adjacency_body(source, target, count, tiles, adj, total):
    total[...] = jnp.zeros_like(total)

    def add_tile(e, carry):
        rows = pl.ds(pl.multiple_of(target[0, e] * BLK, BLK), BLK)
        s = source[0, e]
        total[s, rows, :] = total[s, rows, :] + tiles[e].astype(F32)
        return carry

    lax.fori_loop(0, count[0], add_tile, 0)
    for n in range(5):
        adj[n, :, :BLK] = total[2 * n].astype(BF16)
        adj[n, :, BLK:] = total[2 * n + 1].astype(BF16)


def gate_body(steps, x, cw, cb, gated, dfilt, dgate):
    table = conv_table(cw[0], cw[1])
    bias = cb[...]
    turned = half_turn(bias)
    low = low_lanes(bias.shape)
    bias_f = jnp.where(low, bias, turned)
    bias_g = jnp.where(low, turned, bias)
    for j in range(steps // 2):
        if j == 0:
            pre = dot(x[:, :PAIR], table[PAIR:])
        else:
            pre = dot(x[:, (j - 1) * PAIR : (j + 1) * PAIR], table)
        filt = jnp.tanh(pre[:, :PAIR] + bias_f)
        opened = jax.nn.sigmoid(pre[:, PAIR:] + bias_g)
        cols = slice(j * PAIR, (j + 1) * PAIR)
        both = filt * opened
        gated[:, cols] = both.astype(BF16)
        dfilt[:, cols] = opened * (1.0 - filt * filt)
        dgate[:, cols] = both * (1.0 - opened)


def first_body(adj, g, *outs):
    field = g[...]
    for n, out in zip((3, 4, 1, 2, 0), outs):
        out[...] = dot_tn(adj[n], field).astype(out.dtype)


def second_body(adj, own, p1, p2, p3, p4, u, *outs):
    total = own[...]
    for p in (p1, p2, p3, p4):
        total = total + p[...].astype(F32)
    field = total.astype(BF16)
    u[...] = field
    for n, out in zip((3, 4, 1, 2, 0), outs):
        out[...] = dot_tn(adj[n], field).astype(out.dtype)


def early_body(steps, g, u1, gated, dw, back, sums):
    t0 = diff_table(dw[0])
    t1 = diff_table(dw[1])
    acc = [jnp.zeros((PAIR, PAIR), F32) for _ in range(2)]
    for j in range(steps // 2):
        gj, uj, hj = pairs(g, j), pairs(u1, j), pairs(gated, j)
        back[:, j * PAIR : (j + 1) * PAIR] = dot_nt(gj, t0) + dot_nt(uj, t1)
        acc[0] = acc[0] + dot_tn(hj, gj)
        acc[1] = acc[1] + dot_tn(hj, uj)
    sums[0] = acc[0]
    sums[1] = acc[1]


def fold(q):
    return q[:CH] + half_turn(q[CH:])


def late_body(
    steps, x, gated, dfilt, dgate, own, p1, p2, p3, p4, back, sums, dw, dpre, partial
):
    t2 = diff_table(dw[2])
    half = steps // 2
    acc = jnp.zeros((PAIR, PAIR), F32)
    bias_f = jnp.zeros((1, PAIR), F32)
    bias_g = jnp.zeros((1, PAIR), F32)
    for j in range(half):
        cols = slice(j * PAIR, (j + 1) * PAIR)
        u2 = own[:, cols]
        for p in (p1, p2, p3, p4):
            u2 = u2 + p[:, cols].astype(F32)
        u2 = u2.astype(BF16)
        back_zero = back[:, cols] + dot_nt(u2, t2)
        df = (back_zero * dfilt[:, cols]).astype(BF16)
        dg = (back_zero * dgate[:, cols]).astype(BF16)
        dpre[:, 2 * j * PAIR : (2 * j + 1) * PAIR] = df
        dpre[:, (2 * j + 1) * PAIR : (2 * j + 2) * PAIR] = dg
        acc = acc + dot_tn(pairs(gated, j), u2)
        bias_f = bias_f + jnp.sum(df.astype(F32), axis=0, keepdims=True)
        bias_g = bias_g + jnp.sum(dg.astype(F32), axis=0, keepdims=True)
    here = jnp.zeros((PAIR, 2 * PAIR), F32)
    ahead = jnp.zeros((PAIR, 2 * PAIR), F32)
    for j in range(half):
        xj = pairs(x, j)
        if j + 1 < half:
            prod = dot_tn(xj, dpre[:, 2 * j * PAIR : (2 * j + 4) * PAIR])
            ahead = ahead + prod[:, 2 * PAIR :]
            here = here + prod[:, : 2 * PAIR]
        else:
            here = here + dot_tn(xj, dpre[:, 2 * j * PAIR : (2 * j + 2) * PAIR])
    low = low_lanes((CH, PAIR))
    top_f, top_g = here[:CH, :PAIR], here[:CH, PAIR:]
    bottom_f, bottom_g = here[CH:, :PAIR], here[CH:, PAIR:]
    next_f, next_g = ahead[CH:, :PAIR], ahead[CH:, PAIR:]
    partial[:CH] = jnp.where(low, top_f + half_turn(bottom_f), half_turn(top_g) + bottom_g)
    partial[CH:PAIR] = jnp.where(low, half_turn(top_f) + next_f, top_g + half_turn(next_g))
    q0, q1, q2 = fold(sums[0]), fold(sums[1]), fold(acc)
    partial[DIFF_ROWS : DIFF_ROWS + CH] = jnp.where(low, q0, half_turn(q1))
    partial[DIFF_ROWS + CH : BIAS_ROW] = jnp.where(low[:32], q2[:32], half_turn(q2[32:]))
    bias = jnp.where(
        low[:1], bias_f + half_turn(bias_f), bias_g + half_turn(bias_g)
    )
    row = lax.broadcasted_iota(jnp.int32, (ROWS - BIAS_ROW, PAIR), 0)
    partial[BIAS_ROW:] = jnp.where(row == 0, bias, 0.0)


def features_body(steps, g, dpre, cw, out):
    table = conv_table(cw[0], cw[1])
    here = table[PAIR:]
    ahead = table[:PAIR]
    half = steps // 2
    for j in range(half):
        cols = slice(j * PAIR, (j + 1) * PAIR)
        total = g[:, cols].astype(F32) + dot_nt(dpre[:, 2 * j * PAIR : (2 * j + 2) * PAIR], here)
        if j + 1 < half:
            total = total + dot_nt(dpre[:, (2 * j + 2) * PAIR : (2 * j + 4) * PAIR], ahead)
        out[:, cols] = total.astype(BF16)


def hop_body(adj, own, f1, f2, f3, f4, out):
    total = dot(adj[0], own[...])
    for n, f in ((1, f1), (2, f2), (3, f3), (4, f4)):
        total = total + dot(adj[n], f[...])
    out[...] = total.astype(BF16)


def mix_body(steps, adj, hop1, f1, f2, f3, f4, x, gated, dw, out):
    total = dot(adj[0], hop1[...])
    for n, f in ((1, f1), (2, f2), (3, f3), (4, f4)):
        total = total + dot(adj[n], f[...])
    hop2 = total.astype(BF16)
    t0, t1, t2 = diff_table(dw[0]), diff_table(dw[1]), diff_table(dw[2])
    for j in range(steps // 2):
        cols = slice(j * PAIR, (j + 1) * PAIR)
        mixed = x[:, cols].astype(F32) + dot(gated[:, cols], t0)
        mixed = mixed + dot(hop1[:, cols], t1) + dot(hop2[:, cols], t2)
        out[:, cols] = mixed.astype(BF16)


def finish_body(scale, full, diff, conv, bias):
    conv[0] = full[:CH] * scale
    conv[1] = full[CH:PAIR] * scale
    both = full[DIFF_ROWS : DIFF_ROWS + CH] * scale
    last = full[DIFF_ROWS + CH : BIAS_ROW] * scale
    diff[0] = both[:, :CH]
    diff[1] = half_turn(both)[:, :CH]
    diff[2, :32] = last[:, :CH]
    diff[2, 32:] = half_turn(last)[:, :CH]
    bias[...] = full[BIAS_ROW : BIAS_ROW + 1] * scale


def local(x, g, cw, cb, dw, tiles, source, target, count):
    cells, width = x.shape
    steps = width // CH
    both_axes = ("region", "dom")
    devices = lax.axis_size(both_axes)
    scale = 1.0 / math.sqrt(cells * devices * steps)
    field = ((cells, width), BF16)
    field32 = ((cells, width), F32)
    mac = 2 * cells * width

    (adj,) = call(
        adjacency_body,
        [((5, 2 * BLK, 2 * BLK), BF16)],
        (source, target, count, tiles),
        [SMEM, SMEM, SMEM, VMEM],
        0,
        [pltpu.VMEM((10, 2 * BLK, BLK), F32)],
    )

    def send_back(p3, p4, p1, p2):
        return (
            shift(p1, "dom", -1),
            shift(p2, "dom", 1),
            shift(p3, "region", -1),
            shift(p4, "region", 1),
        )

    def send_out(f):
        return (
            shift(f, "dom", 1),
            shift(f, "dom", -1),
            shift(f, "region", 1),
            shift(f, "region", -1),
        )

    *parts, own = call(
        first_body, [field] * 4 + [field32], (adj, g), [VMEM] * 2, mac * 5 * 2 * BLK
    )
    arrived = send_back(*parts)
    gated, dfilt, dgate = call(
        lambda *r: gate_body(steps, *r),
        [field, field32, field32],
        (x, cw, cb.reshape(1, -1)),
        [VMEM] * 3,
        mac * 2 * PAIR,
    )
    u1, *parts, own = call(
        second_body,
        [field] * 5 + [field32],
        (adj, own, *arrived),
        [VMEM] * 6,
        mac * 5 * 2 * BLK,
    )
    arrived = send_back(*parts)
    back, sums = call(
        lambda *r: early_body(steps, *r),
        [field32, ((2, PAIR, PAIR), F32)],
        (g, u1, gated, dw),
        [VMEM] * 4,
        mac * 4 * PAIR,
    )
    dpre, partial = call(
        lambda *r: late_body(steps, *r),
        [((cells, 2 * width), BF16), ((ROWS, PAIR), F32)],
        (x, gated, dfilt, dgate, own, *arrived, back, sums, dw),
        [VMEM] * 12,
        mac * 6 * PAIR,
    )
    spread = lax.all_to_all(partial, both_axes, 0, 0, tiled=True)
    piece = jnp.sum(spread, axis=0, keepdims=True)
    full = lax.all_to_all(
        jnp.broadcast_to(piece, (ROWS, PAIR)), both_axes, 0, 0, tiled=True
    )

    (grad_features,) = call(
        lambda *r: features_body(steps, *r),
        [field],
        (g, dpre, cw),
        [VMEM] * 3,
        mac * 4 * PAIR,
    )
    (hop1,) = call(
        hop_body, [field], (adj, gated, *send_out(gated)), [VMEM] * 6, mac * 5 * 2 * BLK
    )
    (mixed,) = call(
        lambda *r: mix_body(steps, *r),
        [field],
        (adj, hop1, *send_out(hop1), x, gated, dw),
        [VMEM] * 9,
        mac * 8 * 2 * BLK,
    )
    diff, conv, bias = call(
        lambda *r: finish_body(scale, *r),
        [((3, CH, CH), F32), ((2, CH, PAIR), F32), ((1, PAIR), F32)],
        (full,),
        [VMEM],
        0,
    )
    return mixed, grad_features, diff, conv, bias.reshape(-1)


def solution(mesh):
    split = P(("region", "dom"), None)
    in_specs = (
        split,
        split,
        P(),
        P(),
        P(),
        P(("region", "dom"), None, None),
        split,
        split,
        P(("region", "dom")),
    )
    out_specs = (split, split, P(), P(), P())
    return jax.shard_map(local, mesh=mesh, in_specs=in_specs, out_specs=out_specs, check_vma=False)
```

```python
import math

import jax
import jax.numpy as jnp
from jax import lax
from jax.experimental import pallas as pl
from jax.experimental.pallas import tpu as pltpu
from jax.sharding import PartitionSpec as P

BF16 = jnp.bfloat16
F32 = jnp.float32
CH = 64
PAIR = 2 * CH
BLK = 128
ROWS = 256
DIFF_ROWS = 128
BIAS_ROW = 224

VMEM = pl.BlockSpec(memory_space=pltpu.VMEM)
SMEM = pl.BlockSpec(memory_space=pltpu.SMEM)


DOM = ("x", "z", "c")
ALL = ("r", "x", "z", "c")


def swap(block, axis, first):
    count = lax.axis_size(axis)
    route = []
    for i in range(count):
        step = 1 if i % 2 == first else -1
        route.append((i, (i + step) % count))
    return lax.ppermute(block, axis, route)


def trade(blocks):
    core, cross, even, odd = blocks
    return (
        swap(core, DOM, 0),
        swap(cross, DOM, 1),
        swap(even, "r", 0),
        swap(odd, "r", 1),
    )


def call(body, outs, args, specs, flops, scratch=()):
    moved = sum(a.size * a.dtype.itemsize for a in args)
    moved += sum(math.prod(s) * jnp.dtype(d).itemsize for s, d in outs)
    return pl.pallas_call(
        body,
        out_shape=[jax.ShapeDtypeStruct(s, d) for s, d in outs],
        in_specs=specs,
        out_specs=[VMEM] * len(outs),
        scratch_shapes=list(scratch),
        compiler_params=pltpu.CompilerParams(vmem_limit_bytes=16 * 1024 * 1024),
        cost_estimate=pl.CostEstimate(flops=flops, bytes_accessed=moved, transcendentals=0),
    )(*args)


def dot(a, b):
    return jnp.dot(a, b, preferred_element_type=F32)


def dot_nt(a, b):
    return lax.dot_general(a, b, (((1,), (1,)), ((), ())), preferred_element_type=F32)


def dot_tn(a, b):
    return lax.dot_general(a, b, (((0,), (0,)), ((), ())), preferred_element_type=F32)


def place(rows, cols, offset_of):
    r = lax.broadcasted_iota(jnp.int32, (rows, cols), 0)
    c = lax.broadcasted_iota(jnp.int32, (rows, cols), 1)
    return jnp.where(c == offset_of(r), 1.0, 0.0).astype(BF16)


def low_lanes(shape):
    return lax.broadcasted_iota(jnp.int32, shape, 1) < CH


def half_turn(v):
    return pltpu.roll(v, CH, 1)


def conv_table(w0, w1):
    even = place(PAIR, 2 * PAIR, lambda r: jnp.where(r < CH, r, r + CH))
    odd = place(PAIR, 2 * PAIR, lambda r: jnp.where(r < CH, r + CH, r + PAIR))
    tap1_even = dot(w1, even)
    tap0_even = dot(w0, even)
    tap1_odd = dot(w1, odd)
    tap0_odd = dot(w0, odd)
    rows = [jnp.zeros_like(tap1_even), tap1_even, tap0_even + tap1_odd, tap0_odd]
    return jnp.concatenate(rows, axis=0).astype(BF16)


def diff_table(w):
    low = place(CH, PAIR, lambda r: r)
    high = place(CH, PAIR, lambda r: r + CH)
    return jnp.concatenate([dot(w, low), dot(w, high)], axis=0).astype(BF16)


def pairs(ref, j):
    return ref[:, j * PAIR : (j + 1) * PAIR]


def adjacency_body(source, target, count, tiles, adj, total):
    total[...] = jnp.zeros_like(total)
    odd_core = lax.axis_index("c")
    odd_region = lax.rem(lax.axis_index("r"), 2)

    def add_tile(e, carry):
        rows = pl.ds(pl.multiple_of(target[0, e] * BLK, BLK), BLK)
        s = source[0, e]
        choice = lax.shift_right_logical(s, 1)
        dom_trade = jnp.where(choice == 2 - odd_core, 1, 2)
        region_trade = jnp.where(choice == 4 - odd_region, 3, 4)
        met = jnp.where(choice == 0, 0, jnp.where(choice < 3, dom_trade, region_trade))
        s = 2 * met + lax.bitwise_and(s, 1)
        total[s, rows, :] = total[s, rows, :] + tiles[e].astype(F32)
        return carry

    lax.fori_loop(0, count[0], add_tile, 0)
    for n in range(5):
        adj[n, :, :BLK] = total[2 * n].astype(BF16)
        adj[n, :, BLK:] = total[2 * n + 1].astype(BF16)


def gate_body(steps, x, cw, cb, gated, dfilt, dgate):
    table = conv_table(cw[0], cw[1])
    bias = cb[...]
    turned = half_turn(bias)
    low = low_lanes(bias.shape)
    bias_f = jnp.where(low, bias, turned)
    bias_g = jnp.where(low, turned, bias)
    for j in range(steps // 2):
        if j == 0:
            pre = dot(x[:, :PAIR], table[PAIR:])
        else:
            pre = dot(x[:, (j - 1) * PAIR : (j + 1) * PAIR], table)
        filt = jnp.tanh(pre[:, :PAIR] + bias_f)
        opened = jax.nn.sigmoid(pre[:, PAIR:] + bias_g)
        cols = slice(j * PAIR, (j + 1) * PAIR)
        both = filt * opened
        gated[:, cols] = both.astype(BF16)
        dfilt[:, cols] = opened * (1.0 - filt * filt)
        dgate[:, cols] = both * (1.0 - opened)


def first_body(adj, g, *outs):
    field = g[...]
    for n, out in zip((1, 2, 3, 4, 0), outs):
        out[...] = dot_tn(adj[n], field).astype(out.dtype)


def second_body(adj, own, p1, p2, p3, p4, u, *outs):
    total = own[...]
    for p in (p1, p2, p3, p4):
        total = total + p[...].astype(F32)
    field = total.astype(BF16)
    u[...] = field
    for n, out in zip((1, 2, 3, 4, 0), outs):
        out[...] = dot_tn(adj[n], field).astype(out.dtype)


def early_body(steps, g, u1, gated, dw, back, sums):
    t0 = diff_table(dw[0])
    t1 = diff_table(dw[1])
    acc = [jnp.zeros((PAIR, PAIR), F32) for _ in range(2)]
    for j in range(steps // 2):
        gj, uj, hj = pairs(g, j), pairs(u1, j), pairs(gated, j)
        back[:, j * PAIR : (j + 1) * PAIR] = dot_nt(gj, t0) + dot_nt(uj, t1)
        acc[0] = acc[0] + dot_tn(hj, gj)
        acc[1] = acc[1] + dot_tn(hj, uj)
    sums[0] = acc[0]
    sums[1] = acc[1]


def fold(q):
    return q[:CH] + half_turn(q[CH:])


def late_body(
    steps, x, gated, dfilt, dgate, own, p1, p2, p3, p4, back, sums, dw, dpre, partial
):
    t2 = diff_table(dw[2])
    half = steps // 2
    acc = jnp.zeros((PAIR, PAIR), F32)
    bias_f = jnp.zeros((1, PAIR), F32)
    bias_g = jnp.zeros((1, PAIR), F32)
    for j in range(half):
        cols = slice(j * PAIR, (j + 1) * PAIR)
        u2 = own[:, cols]
        for p in (p1, p2, p3, p4):
            u2 = u2 + p[:, cols].astype(F32)
        u2 = u2.astype(BF16)
        back_zero = back[:, cols] + dot_nt(u2, t2)
        df = (back_zero * dfilt[:, cols]).astype(BF16)
        dg = (back_zero * dgate[:, cols]).astype(BF16)
        dpre[:, 2 * j * PAIR : (2 * j + 1) * PAIR] = df
        dpre[:, (2 * j + 1) * PAIR : (2 * j + 2) * PAIR] = dg
        acc = acc + dot_tn(pairs(gated, j), u2)
        bias_f = bias_f + jnp.sum(df.astype(F32), axis=0, keepdims=True)
        bias_g = bias_g + jnp.sum(dg.astype(F32), axis=0, keepdims=True)
    here = jnp.zeros((PAIR, 2 * PAIR), F32)
    ahead = jnp.zeros((PAIR, 2 * PAIR), F32)
    for j in range(half):
        xj = pairs(x, j)
        if j + 1 < half:
            prod = dot_tn(xj, dpre[:, 2 * j * PAIR : (2 * j + 4) * PAIR])
            ahead = ahead + prod[:, 2 * PAIR :]
            here = here + prod[:, : 2 * PAIR]
        else:
            here = here + dot_tn(xj, dpre[:, 2 * j * PAIR : (2 * j + 2) * PAIR])
    low = low_lanes((CH, PAIR))
    top_f, top_g = here[:CH, :PAIR], here[:CH, PAIR:]
    bottom_f, bottom_g = here[CH:, :PAIR], here[CH:, PAIR:]
    next_f, next_g = ahead[CH:, :PAIR], ahead[CH:, PAIR:]
    partial[:CH] = jnp.where(low, top_f + half_turn(bottom_f), half_turn(top_g) + bottom_g)
    partial[CH:PAIR] = jnp.where(low, half_turn(top_f) + next_f, top_g + half_turn(next_g))
    q0, q1, q2 = fold(sums[0]), fold(sums[1]), fold(acc)
    partial[DIFF_ROWS : DIFF_ROWS + CH] = jnp.where(low, q0, half_turn(q1))
    partial[DIFF_ROWS + CH : BIAS_ROW] = jnp.where(low[:32], q2[:32], half_turn(q2[32:]))
    bias = jnp.where(
        low[:1], bias_f + half_turn(bias_f), bias_g + half_turn(bias_g)
    )
    row = lax.broadcasted_iota(jnp.int32, (ROWS - BIAS_ROW, PAIR), 0)
    partial[BIAS_ROW:] = jnp.where(row == 0, bias, 0.0)


def features_body(steps, g, dpre, cw, out):
    table = conv_table(cw[0], cw[1])
    here = table[PAIR:]
    ahead = table[:PAIR]
    half = steps // 2
    for j in range(half):
        cols = slice(j * PAIR, (j + 1) * PAIR)
        total = g[:, cols].astype(F32) + dot_nt(dpre[:, 2 * j * PAIR : (2 * j + 2) * PAIR], here)
        if j + 1 < half:
            total = total + dot_nt(dpre[:, (2 * j + 2) * PAIR : (2 * j + 4) * PAIR], ahead)
        out[:, cols] = total.astype(BF16)


def hop_body(adj, own, f1, f2, f3, f4, out):
    total = dot(adj[0], own[...])
    for n, f in ((1, f1), (2, f2), (3, f3), (4, f4)):
        total = total + dot(adj[n], f[...])
    out[...] = total.astype(BF16)


def mix_body(steps, adj, hop1, f1, f2, f3, f4, x, gated, dw, out):
    total = dot(adj[0], hop1[...])
    for n, f in ((1, f1), (2, f2), (3, f3), (4, f4)):
        total = total + dot(adj[n], f[...])
    hop2 = total.astype(BF16)
    t0, t1, t2 = diff_table(dw[0]), diff_table(dw[1]), diff_table(dw[2])
    for j in range(steps // 2):
        cols = slice(j * PAIR, (j + 1) * PAIR)
        mixed = x[:, cols].astype(F32) + dot(gated[:, cols], t0)
        mixed = mixed + dot(hop1[:, cols], t1) + dot(hop2[:, cols], t2)
        out[:, cols] = mixed.astype(BF16)


def finish_body(scale, full, diff, conv, bias):
    conv[0] = full[:CH] * scale
    conv[1] = full[CH:PAIR] * scale
    both = full[DIFF_ROWS : DIFF_ROWS + CH] * scale
    last = full[DIFF_ROWS + CH : BIAS_ROW] * scale
    diff[0] = both[:, :CH]
    diff[1] = half_turn(both)[:, :CH]
    diff[2, :32] = last[:, :CH]
    diff[2, 32:] = half_turn(last)[:, :CH]
    bias[...] = full[BIAS_ROW : BIAS_ROW + 1] * scale


def local(x, g, cw, cb, dw, tiles, source, target, count):
    cells, width = x.shape
    steps = width // CH
    devices = lax.axis_size(ALL)
    scale = 1.0 / math.sqrt(cells * devices * steps)
    field = ((cells, width), BF16)
    field32 = ((cells, width), F32)
    mac = 2 * cells * width

    (adj,) = call(
        adjacency_body,
        [((5, 2 * BLK, 2 * BLK), BF16)],
        (source, target, count, tiles),
        [SMEM, SMEM, SMEM, VMEM],
        0,
        [pltpu.VMEM((10, 2 * BLK, BLK), F32)],
    )

    *parts, own = call(
        first_body, [field] * 4 + [field32], (adj, g), [VMEM] * 2, mac * 5 * 2 * BLK
    )
    arrived = trade(parts)
    gated, dfilt, dgate = call(
        lambda *r: gate_body(steps, *r),
        [field, field32, field32],
        (x, cw, cb.reshape(1, -1)),
        [VMEM] * 3,
        mac * 2 * PAIR,
    )
    u1, *parts, own = call(
        second_body,
        [field] * 5 + [field32],
        (adj, own, *arrived),
        [VMEM] * 6,
        mac * 5 * 2 * BLK,
    )
    arrived = trade(parts)
    back, sums = call(
        lambda *r: early_body(steps, *r),
        [field32, ((2, PAIR, PAIR), F32)],
        (g, u1, gated, dw),
        [VMEM] * 4,
        mac * 4 * PAIR,
    )
    dpre, partial = call(
        lambda *r: late_body(steps, *r),
        [((cells, 2 * width), BF16), ((ROWS, PAIR), F32)],
        (x, gated, dfilt, dgate, own, *arrived, back, sums, dw),
        [VMEM] * 12,
        mac * 6 * PAIR,
    )
    plane, depth = ("r", "x", "c"), lax.axis_size("z")
    width_p = lax.axis_size(plane)
    rows = ROWS // width_p
    piece = lax.all_to_all(partial.reshape(width_p, rows, PAIR), plane, 0, 0, tiled=True)
    piece = jnp.broadcast_to(jnp.sum(piece, axis=0), (depth, rows, PAIR))
    piece = jnp.sum(lax.all_to_all(piece, "z", 0, 0, tiled=True), axis=0)
    piece = jnp.broadcast_to(piece, (width_p, rows, PAIR))
    full = lax.all_to_all(piece, plane, 0, 0, tiled=True).reshape(ROWS, PAIR)

    (grad_features,) = call(
        lambda *r: features_body(steps, *r),
        [field],
        (g, dpre, cw),
        [VMEM] * 3,
        mac * 4 * PAIR,
    )
    (hop1,) = call(
        hop_body, [field], (adj, gated, *trade([gated] * 4)), [VMEM] * 6, mac * 5 * 2 * BLK
    )
    (mixed,) = call(
        lambda *r: mix_body(steps, *r),
        [field],
        (adj, hop1, *trade([hop1] * 4), x, gated, dw),
        [VMEM] * 9,
        mac * 8 * 2 * BLK,
    )
    diff, conv, bias = call(
        lambda *r: finish_body(scale, *r),
        [((3, CH, CH), F32), ((2, CH, PAIR), F32), ((1, PAIR), F32)],
        (full,),
        [VMEM],
        0,
    )
    return mixed, grad_features, diff, conv, bias.reshape(-1)


def solution(mesh):
    region, dom = mesh.devices.shape
    grid = mesh.devices.reshape(region, dom // 16, 8, 2)
    split = P(ALL, None)
    in_specs = (split, split, P(), P(), P(), P(ALL, None, None), split, split, P(ALL))
    out_specs = (split, split, P(), P(), P())
    return jax.shard_map(
        local,
        mesh=jax.sharding.Mesh(grid, ALL),
        in_specs=in_specs,
        out_specs=out_specs,
        check_vma=False,
    )
```

```python
import math

import jax
import jax.numpy as jnp
from jax import lax
from jax.experimental import pallas as pl
from jax.experimental.pallas import tpu as pltpu
from jax.sharding import PartitionSpec as P

BF16 = jnp.bfloat16
F32 = jnp.float32
CH = 64
PAIR = 2 * CH
BLK = 128
ROWS = 256
DIFF_ROWS = 128
BIAS_ROW = 224
HOP1_ORDER = (3, 4, 1, 2)
HOP2_ORDER = (3, 4, 1, 2)
BACK2_ORDER = (3, 4, 1, 2)
BACK1_ORDER = (1, 2, 3, 4)

VMEM = pl.BlockSpec(memory_space=pltpu.VMEM)
SMEM = pl.BlockSpec(memory_space=pltpu.SMEM)
AFTER = pl.BlockSpec(memory_space=pl.ANY)


DOM = ("x", "z", "c")
ALL = ("r", "x", "z", "c")


def swap(block, axis, first):
    count = lax.axis_size(axis)
    route = []
    for i in range(count):
        step = 1 if i % 2 == first else -1
        route.append((i, (i + step) % count))
    return lax.ppermute(block, axis, route)


def trade(blocks):
    core, cross, even, odd = blocks
    return (
        swap(core, DOM, 0),
        swap(cross, DOM, 1),
        swap(even, "r", 0),
        swap(odd, "r", 1),
    )


def ordered(arrived, order):
    return [arrived[k - 1] for k in order]


def call(body, outs, args, specs, flops, scratch=()):
    moved = sum(a.size * a.dtype.itemsize for a in args)
    moved += sum(math.prod(s) * jnp.dtype(d).itemsize for s, d in outs)
    return pl.pallas_call(
        body,
        out_shape=[jax.ShapeDtypeStruct(s, d) for s, d in outs],
        in_specs=specs,
        out_specs=[VMEM] * len(outs),
        scratch_shapes=list(scratch),
        compiler_params=pltpu.CompilerParams(vmem_limit_bytes=16 * 1024 * 1024),
        cost_estimate=pl.CostEstimate(flops=flops, bytes_accessed=moved, transcendentals=0),
    )(*args)


def dot(a, b):
    return jnp.dot(a, b, preferred_element_type=F32)


def dot_nt(a, b):
    return lax.dot_general(a, b, (((1,), (1,)), ((), ())), preferred_element_type=F32)


def dot_tn(a, b):
    return lax.dot_general(a, b, (((0,), (0,)), ((), ())), preferred_element_type=F32)


def place(rows, cols, offset_of):
    r = lax.broadcasted_iota(jnp.int32, (rows, cols), 0)
    c = lax.broadcasted_iota(jnp.int32, (rows, cols), 1)
    return jnp.where(c == offset_of(r), 1.0, 0.0).astype(BF16)


def low_lanes(shape):
    return lax.broadcasted_iota(jnp.int32, shape, 1) < CH


def half_turn(v):
    return pltpu.roll(v, CH, 1)


def conv_table(w0, w1):
    even = place(PAIR, 2 * PAIR, lambda r: jnp.where(r < CH, r, r + CH))
    odd = place(PAIR, 2 * PAIR, lambda r: jnp.where(r < CH, r + CH, r + PAIR))
    tap1_even = dot(w1, even)
    tap0_even = dot(w0, even)
    tap1_odd = dot(w1, odd)
    tap0_odd = dot(w0, odd)
    rows = [jnp.zeros_like(tap1_even), tap1_even, tap0_even + tap1_odd, tap0_odd]
    return jnp.concatenate(rows, axis=0).astype(BF16)


def diff_table(w):
    low = place(CH, PAIR, lambda r: r)
    high = place(CH, PAIR, lambda r: r + CH)
    return jnp.concatenate([dot(w, low), dot(w, high)], axis=0).astype(BF16)


def pairs(ref, j):
    return ref[:, j * PAIR : (j + 1) * PAIR]


def adjacency_body(source, target, count, tiles, adj, total):
    total[...] = jnp.zeros_like(total)
    odd_core = lax.axis_index("c")
    odd_region = lax.rem(lax.axis_index("r"), 2)

    def add_tile(e, carry):
        rows = pl.ds(pl.multiple_of(target[0, e] * BLK, BLK), BLK)
        s = source[0, e]
        choice = lax.shift_right_logical(s, 1)
        dom_trade = jnp.where(choice == 2 - odd_core, 1, 2)
        region_trade = jnp.where(choice == 4 - odd_region, 3, 4)
        met = jnp.where(choice == 0, 0, jnp.where(choice < 3, dom_trade, region_trade))
        s = 2 * met + lax.bitwise_and(s, 1)
        total[s, rows, :] = total[s, rows, :] + tiles[e].astype(F32)
        return carry

    lax.fori_loop(0, count[0], add_tile, 0)
    for n in range(5):
        adj[n, :, :BLK] = total[2 * n].astype(BF16)
        adj[n, :, BLK:] = total[2 * n + 1].astype(BF16)


def gate_body(steps, x, cw, cb, gated, dfilt, dgate):
    table = conv_table(cw[0], cw[1])
    bias = cb[...]
    turned = half_turn(bias)
    low = low_lanes(bias.shape)
    bias_f = jnp.where(low, bias, turned)
    bias_g = jnp.where(low, turned, bias)
    for j in range(steps // 2):
        if j == 0:
            pre = dot(x[:, :PAIR], table[PAIR:])
        else:
            pre = dot(x[:, (j - 1) * PAIR : (j + 1) * PAIR], table)
        filt = jnp.tanh(pre[:, :PAIR] + bias_f)
        opened = jax.nn.sigmoid(pre[:, PAIR:] + bias_g)
        cols = slice(j * PAIR, (j + 1) * PAIR)
        both = filt * opened
        gated[:, cols] = both.astype(BF16)
        dfilt[:, cols] = opened * (1.0 - filt * filt)
        dgate[:, cols] = both * (1.0 - opened)


def first_body(adj, g, *outs):
    field = g[...]
    for n, out in zip((1, 2, 3, 4, 0), outs):
        out[...] = dot_tn(adj[n], field).astype(out.dtype)


def second_body(adj, own, p1, p2, p3, p4, u, *outs):
    total = own[...]
    for p in (p1, p2, p3, p4):
        total = total + p[...].astype(F32)
    field = total.astype(BF16)
    u[...] = field
    for n, out in zip((1, 2, 3, 4, 0), outs):
        out[...] = dot_tn(adj[n], field).astype(out.dtype)


def early_body(steps, g, u1, gated, dw, back, sums):
    t0 = diff_table(dw[0])
    t1 = diff_table(dw[1])
    acc = [jnp.zeros((PAIR, PAIR), F32) for _ in range(2)]
    for j in range(steps // 2):
        gj, uj, hj = pairs(g, j), pairs(u1, j), pairs(gated, j)
        back[:, j * PAIR : (j + 1) * PAIR] = dot_nt(gj, t0) + dot_nt(uj, t1)
        acc[0] = acc[0] + dot_tn(hj, gj)
        acc[1] = acc[1] + dot_tn(hj, uj)
    sums[0] = acc[0]
    sums[1] = acc[1]


def fold(q):
    return q[:CH] + half_turn(q[CH:])


def late_body(
    steps, x, gated, dfilt, dgate, own, p1, p2, p3, p4, back, sums, dw, dpre, partial
):
    t2 = diff_table(dw[2])
    half = steps // 2
    acc = jnp.zeros((PAIR, PAIR), F32)
    bias_f = jnp.zeros((1, PAIR), F32)
    bias_g = jnp.zeros((1, PAIR), F32)
    for j in range(half):
        cols = slice(j * PAIR, (j + 1) * PAIR)
        u2 = own[:, cols]
        for p in (p1, p2, p3, p4):
            u2 = u2 + p[:, cols].astype(F32)
        u2 = u2.astype(BF16)
        back_zero = back[:, cols] + dot_nt(u2, t2)
        df = (back_zero * dfilt[:, cols]).astype(BF16)
        dg = (back_zero * dgate[:, cols]).astype(BF16)
        dpre[:, 2 * j * PAIR : (2 * j + 1) * PAIR] = df
        dpre[:, (2 * j + 1) * PAIR : (2 * j + 2) * PAIR] = dg
        acc = acc + dot_tn(pairs(gated, j), u2)
        bias_f = bias_f + jnp.sum(df.astype(F32), axis=0, keepdims=True)
        bias_g = bias_g + jnp.sum(dg.astype(F32), axis=0, keepdims=True)
    here = jnp.zeros((PAIR, 2 * PAIR), F32)
    ahead = jnp.zeros((PAIR, 2 * PAIR), F32)
    for j in range(half):
        xj = pairs(x, j)
        if j + 1 < half:
            prod = dot_tn(xj, dpre[:, 2 * j * PAIR : (2 * j + 4) * PAIR])
            ahead = ahead + prod[:, 2 * PAIR :]
            here = here + prod[:, : 2 * PAIR]
        else:
            here = here + dot_tn(xj, dpre[:, 2 * j * PAIR : (2 * j + 2) * PAIR])
    low = low_lanes((CH, PAIR))
    top_f, top_g = here[:CH, :PAIR], here[:CH, PAIR:]
    bottom_f, bottom_g = here[CH:, :PAIR], here[CH:, PAIR:]
    next_f, next_g = ahead[CH:, :PAIR], ahead[CH:, PAIR:]
    partial[:CH] = jnp.where(low, top_f + half_turn(bottom_f), half_turn(top_g) + bottom_g)
    partial[CH:PAIR] = jnp.where(low, half_turn(top_f) + next_f, top_g + half_turn(next_g))
    q0, q1, q2 = fold(sums[0]), fold(sums[1]), fold(acc)
    partial[DIFF_ROWS : DIFF_ROWS + CH] = jnp.where(low, q0, half_turn(q1))
    partial[DIFF_ROWS + CH : BIAS_ROW] = jnp.where(low[:32], q2[:32], half_turn(q2[32:]))
    bias = jnp.where(
        low[:1], bias_f + half_turn(bias_f), bias_g + half_turn(bias_g)
    )
    row = lax.broadcasted_iota(jnp.int32, (ROWS - BIAS_ROW, PAIR), 0)
    partial[BIAS_ROW:] = jnp.where(row == 0, bias, 0.0)


def features_body(steps, g, dpre, cw, out):
    table = conv_table(cw[0], cw[1])
    here = table[PAIR:]
    ahead = table[:PAIR]
    half = steps // 2
    for j in range(half):
        cols = slice(j * PAIR, (j + 1) * PAIR)
        total = g[:, cols].astype(F32) + dot_nt(dpre[:, 2 * j * PAIR : (2 * j + 2) * PAIR], here)
        if j + 1 < half:
            total = total + dot_nt(dpre[:, (2 * j + 2) * PAIR : (2 * j + 4) * PAIR], ahead)
        out[:, cols] = total.astype(BF16)


def hop_body(adj, own, f1, f2, f3, f4, out):
    total = dot(adj[0], own[...])
    for n, f in zip(HOP1_ORDER, (f1, f2, f3, f4)):
        total = total + dot(adj[n], f[...])
    out[...] = total.astype(BF16)


def mix_body(steps, adj, hop1, f1, f2, f3, f4, x, gated, dw, out):
    total = dot(adj[0], hop1[...])
    for n, f in zip(HOP2_ORDER, (f1, f2, f3, f4)):
        total = total + dot(adj[n], f[...])
    hop2 = total.astype(BF16)
    t0, t1, t2 = diff_table(dw[0]), diff_table(dw[1]), diff_table(dw[2])
    for j in range(steps // 2):
        cols = slice(j * PAIR, (j + 1) * PAIR)
        mixed = x[:, cols].astype(F32) + dot(gated[:, cols], t0)
        mixed = mixed + dot(hop1[:, cols], t1) + dot(hop2[:, cols], t2)
        out[:, cols] = mixed.astype(BF16)


def finish_body(scale, full, diff, conv, bias):
    conv[0] = full[:CH] * scale
    conv[1] = full[CH:PAIR] * scale
    both = full[DIFF_ROWS : DIFF_ROWS + CH] * scale
    last = full[DIFF_ROWS + CH : BIAS_ROW] * scale
    diff[0] = both[:, :CH]
    diff[1] = half_turn(both)[:, :CH]
    diff[2, :32] = last[:, :CH]
    diff[2, 32:] = half_turn(last)[:, :CH]
    bias[...] = full[BIAS_ROW : BIAS_ROW + 1] * scale


def local(x, g, cw, cb, dw, tiles, source, target, count):
    cells, width = x.shape
    steps = width // CH
    devices = lax.axis_size(ALL)
    scale = 1.0 / math.sqrt(cells * devices * steps)
    field = ((cells, width), BF16)
    field32 = ((cells, width), F32)
    mac = 2 * cells * width

    (adj,) = call(
        adjacency_body,
        [((5, 2 * BLK, 2 * BLK), BF16)],
        (source, target, count, tiles),
        [SMEM, SMEM, SMEM, VMEM],
        0,
        [pltpu.VMEM((10, 2 * BLK, BLK), F32)],
    )

    *parts, own = call(
        first_body, [field] * 4 + [field32], (adj, g), [VMEM] * 2, mac * 5 * 2 * BLK
    )
    arrived = trade(parts)
    gated, dfilt, dgate = call(
        lambda *r: gate_body(steps, *r),
        [field, field32, field32],
        (x, cw, cb.reshape(1, -1)),
        [VMEM] * 3,
        mac * 2 * PAIR,
    )
    u1, *parts, own = call(
        second_body,
        [field] * 5 + [field32],
        (adj, own, *ordered(arrived, BACK1_ORDER)),
        [VMEM] * 6,
        mac * 5 * 2 * BLK,
    )
    arrived = trade(parts)
    back, sums = call(
        lambda *r: early_body(steps, *r),
        [field32, ((2, PAIR, PAIR), F32)],
        (g, u1, gated, dw),
        [VMEM] * 4,
        mac * 4 * PAIR,
    )
    dpre, partial = call(
        lambda *r: late_body(steps, *r),
        [((cells, 2 * width), BF16), ((ROWS, PAIR), F32)],
        (x, gated, dfilt, dgate, own, *ordered(arrived, BACK2_ORDER), back, sums, dw),
        [VMEM] * 12,
        mac * 6 * PAIR,
    )
    plane, depth = ("r", "x", "c"), lax.axis_size("z")
    width_p = lax.axis_size(plane)
    rows = ROWS // width_p
    piece = lax.all_to_all(partial.reshape(width_p, rows, PAIR), plane, 0, 0, tiled=True)
    piece = jnp.broadcast_to(jnp.sum(piece, axis=0), (depth, rows, PAIR))
    piece = jnp.sum(lax.all_to_all(piece, "z", 0, 0, tiled=True), axis=0)
    piece = jnp.broadcast_to(piece, (width_p, rows, PAIR))
    full = lax.all_to_all(piece, plane, 0, 0, tiled=True).reshape(ROWS, PAIR)

    (grad_features,) = call(
        lambda *r: features_body(steps, *r),
        [field],
        (g, dpre, cw),
        [VMEM] * 3,
        mac * 4 * PAIR,
    )
    (hop1,) = call(
        hop_body, [field], (adj, gated, *ordered(trade([gated] * 4), HOP1_ORDER)), [VMEM] * 6, mac * 5 * 2 * BLK
    )
    (mixed,) = call(
        lambda *r: mix_body(steps, *r),
        [field],
        (adj, hop1, *ordered(trade([hop1] * 4), HOP2_ORDER), x, gated, dw),
        [VMEM] * 9,
        mac * 8 * 2 * BLK,
    )
    diff, conv, bias = call(
        lambda *r: finish_body(scale, *r),
        [((3, CH, CH), F32), ((2, CH, PAIR), F32), ((1, PAIR), F32)],
        (full,),
        [VMEM],
        0,
    )
    return mixed, grad_features, diff, conv, bias.reshape(-1)


def solution(mesh):
    region, dom = mesh.devices.shape
    grid = mesh.devices.reshape(region, dom // 16, 8, 2)
    split = P(ALL, None)
    in_specs = (split, split, P(), P(), P(), P(ALL, None, None), split, split, P(ALL))
    out_specs = (split, split, P(), P(), P())
    return jax.shard_map(
        local,
        mesh=jax.sharding.Mesh(grid, ALL),
        in_specs=in_specs,
        out_specs=out_specs,
        check_vma=False,
    )
```

```python
import math

import jax
import jax.numpy as jnp
from jax import lax
from jax.experimental import pallas as pl
from jax.experimental.pallas import tpu as pltpu
from jax.sharding import PartitionSpec as P

BF16 = jnp.bfloat16
F32 = jnp.float32
CH = 64
PAIR = 2 * CH
BLK = 128
ROWS = 256
DIFF_ROWS = 128
BIAS_ROW = 224
HOP1_ORDER = (3, 4, 1, 2)
HOP2_ORDER = (3, 4, 1, 2)
BACK2_ORDER = (3, 4, 1, 2)
BACK1_ORDER = (1, 2, 3, 4)

VMEM = pl.BlockSpec(memory_space=pltpu.VMEM)
SMEM = pl.BlockSpec(memory_space=pltpu.SMEM)
AFTER = pl.BlockSpec(memory_space=pl.ANY)


DOM = ("x", "z", "c")
ALL = ("r", "x", "z", "c")


def swap(block, axis, first):
    count = lax.axis_size(axis)
    route = []
    for i in range(count):
        step = 1 if i % 2 == first else -1
        route.append((i, (i + step) % count))
    return lax.ppermute(block, axis, route)


def trade(blocks):
    core, cross, even, odd = blocks
    return (
        swap(core, DOM, 0),
        swap(cross, DOM, 1),
        swap(even, "r", 0),
        swap(odd, "r", 1),
    )


def ordered(arrived, order):
    return [arrived[k - 1] for k in order]


def call(body, outs, args, specs, flops, scratch=()):
    moved = sum(a.size * a.dtype.itemsize for a in args)
    moved += sum(math.prod(s) * jnp.dtype(d).itemsize for s, d in outs)
    return pl.pallas_call(
        body,
        out_shape=[jax.ShapeDtypeStruct(s, d) for s, d in outs],
        in_specs=specs,
        out_specs=[VMEM] * len(outs),
        scratch_shapes=list(scratch),
        compiler_params=pltpu.CompilerParams(vmem_limit_bytes=16 * 1024 * 1024),
        cost_estimate=pl.CostEstimate(flops=flops, bytes_accessed=moved, transcendentals=0),
    )(*args)


def dot(a, b):
    return jnp.dot(a, b, preferred_element_type=F32)


def dot_nt(a, b):
    return lax.dot_general(a, b, (((1,), (1,)), ((), ())), preferred_element_type=F32)


def dot_tn(a, b):
    return lax.dot_general(a, b, (((0,), (0,)), ((), ())), preferred_element_type=F32)


def place(rows, cols, offset_of):
    r = lax.broadcasted_iota(jnp.int32, (rows, cols), 0)
    c = lax.broadcasted_iota(jnp.int32, (rows, cols), 1)
    return jnp.where(c == offset_of(r), 1.0, 0.0).astype(BF16)


def low_lanes(shape):
    return lax.broadcasted_iota(jnp.int32, shape, 1) < CH


def half_turn(v):
    return pltpu.roll(v, CH, 1)


def conv_table(w0, w1):
    even = place(PAIR, 2 * PAIR, lambda r: jnp.where(r < CH, r, r + CH))
    odd = place(PAIR, 2 * PAIR, lambda r: jnp.where(r < CH, r + CH, r + PAIR))
    tap1_even = dot(w1, even)
    tap0_even = dot(w0, even)
    tap1_odd = dot(w1, odd)
    tap0_odd = dot(w0, odd)
    rows = [jnp.zeros_like(tap1_even), tap1_even, tap0_even + tap1_odd, tap0_odd]
    return jnp.concatenate(rows, axis=0).astype(BF16)


def diff_table(w):
    low = place(CH, PAIR, lambda r: r)
    high = place(CH, PAIR, lambda r: r + CH)
    return jnp.concatenate([dot(w, low), dot(w, high)], axis=0).astype(BF16)


def pairs(ref, j):
    return ref[:, j * PAIR : (j + 1) * PAIR]


def adjacency_body(source, target, count, tiles, adj, total):
    total[...] = jnp.zeros_like(total)
    odd_core = lax.axis_index("c")
    odd_region = lax.rem(lax.axis_index("r"), 2)

    def add_tile(e, carry):
        rows = pl.ds(pl.multiple_of(target[0, e] * BLK, BLK), BLK)
        s = source[0, e]
        choice = lax.shift_right_logical(s, 1)
        dom_trade = jnp.where(choice == 2 - odd_core, 1, 2)
        region_trade = jnp.where(choice == 4 - odd_region, 3, 4)
        met = jnp.where(choice == 0, 0, jnp.where(choice < 3, dom_trade, region_trade))
        s = 2 * met + lax.bitwise_and(s, 1)
        total[s, rows, :] = total[s, rows, :] + tiles[e].astype(F32)
        return carry

    lax.fori_loop(0, count[0], add_tile, 0)
    for n in range(5):
        adj[n, :, :BLK] = total[2 * n].astype(BF16)
        adj[n, :, BLK:] = total[2 * n + 1].astype(BF16)


def gate_body(steps, x, cw, cb, g, dw, gated, dfilt, dgate, back, sums):
    t0 = diff_table(dw[0])
    acc = jnp.zeros((PAIR, PAIR), F32)
    table = conv_table(cw[0], cw[1])
    bias = cb[...]
    turned = half_turn(bias)
    low = low_lanes(bias.shape)
    bias_f = jnp.where(low, bias, turned)
    bias_g = jnp.where(low, turned, bias)
    for j in range(steps // 2):
        if j == 0:
            pre = dot(x[:, :PAIR], table[PAIR:])
        else:
            pre = dot(x[:, (j - 1) * PAIR : (j + 1) * PAIR], table)
        filt = jnp.tanh(pre[:, :PAIR] + bias_f)
        opened = jax.nn.sigmoid(pre[:, PAIR:] + bias_g)
        cols = slice(j * PAIR, (j + 1) * PAIR)
        both = filt * opened
        hj = both.astype(BF16)
        gated[:, cols] = hj
        back[:, cols] = dot_nt(g[:, cols], t0)
        acc = acc + dot_tn(hj, g[:, cols])
        dfilt[:, cols] = opened * (1.0 - filt * filt)
        dgate[:, cols] = both * (1.0 - opened)
    sums[...] = acc


def first_body(adj, g, *outs):
    field = g[...]
    for n, out in zip((1, 2, 3, 4, 0), outs):
        out[...] = dot_tn(adj[n], field).astype(out.dtype)


def second_body(adj, own, p1, p2, p3, p4, u, *outs):
    total = own[...]
    for p in (p1, p2, p3, p4):
        total = total + p[...].astype(F32)
    field = total.astype(BF16)
    u[...] = field
    for n, out in zip((1, 2, 3, 4, 0), outs):
        out[...] = dot_tn(adj[n], field).astype(out.dtype)


def fold(q):
    return q[:CH] + half_turn(q[CH:])


def late_body(
    steps, x, gated, dfilt, dgate, own, p1, p2, p3, p4, back, sums, dw, u1, dpre, partial
):
    t1, t2 = diff_table(dw[1]), diff_table(dw[2])
    half = steps // 2
    acc = jnp.zeros((PAIR, PAIR), F32)
    acc1 = jnp.zeros((PAIR, PAIR), F32)
    bias_f = jnp.zeros((1, PAIR), F32)
    bias_g = jnp.zeros((1, PAIR), F32)
    for j in range(half):
        cols = slice(j * PAIR, (j + 1) * PAIR)
        u2 = own[:, cols]
        for p in (p1, p2, p3, p4):
            u2 = u2 + p[:, cols].astype(F32)
        u2 = u2.astype(BF16)
        back_zero = back[:, cols] + dot_nt(pairs(u1, j), t1) + dot_nt(u2, t2)
        acc1 = acc1 + dot_tn(pairs(gated, j), pairs(u1, j))
        df = (back_zero * dfilt[:, cols]).astype(BF16)
        dg = (back_zero * dgate[:, cols]).astype(BF16)
        dpre[:, 2 * j * PAIR : (2 * j + 1) * PAIR] = df
        dpre[:, (2 * j + 1) * PAIR : (2 * j + 2) * PAIR] = dg
        acc = acc + dot_tn(pairs(gated, j), u2)
        bias_f = bias_f + jnp.sum(df.astype(F32), axis=0, keepdims=True)
        bias_g = bias_g + jnp.sum(dg.astype(F32), axis=0, keepdims=True)
    here = jnp.zeros((PAIR, 2 * PAIR), F32)
    ahead = jnp.zeros((PAIR, 2 * PAIR), F32)
    for j in range(half):
        xj = pairs(x, j)
        if j + 1 < half:
            prod = dot_tn(xj, dpre[:, 2 * j * PAIR : (2 * j + 4) * PAIR])
            ahead = ahead + prod[:, 2 * PAIR :]
            here = here + prod[:, : 2 * PAIR]
        else:
            here = here + dot_tn(xj, dpre[:, 2 * j * PAIR : (2 * j + 2) * PAIR])
    low = low_lanes((CH, PAIR))
    top_f, top_g = here[:CH, :PAIR], here[:CH, PAIR:]
    bottom_f, bottom_g = here[CH:, :PAIR], here[CH:, PAIR:]
    next_f, next_g = ahead[CH:, :PAIR], ahead[CH:, PAIR:]
    partial[:CH] = jnp.where(low, top_f + half_turn(bottom_f), half_turn(top_g) + bottom_g)
    partial[CH:PAIR] = jnp.where(low, half_turn(top_f) + next_f, top_g + half_turn(next_g))
    q0, q1, q2 = fold(sums[...]), fold(acc1), fold(acc)
    partial[DIFF_ROWS : DIFF_ROWS + CH] = jnp.where(low, q0, half_turn(q1))
    partial[DIFF_ROWS + CH : BIAS_ROW] = jnp.where(low[:32], q2[:32], half_turn(q2[32:]))
    bias = jnp.where(
        low[:1], bias_f + half_turn(bias_f), bias_g + half_turn(bias_g)
    )
    row = lax.broadcasted_iota(jnp.int32, (ROWS - BIAS_ROW, PAIR), 0)
    partial[BIAS_ROW:] = jnp.where(row == 0, bias, 0.0)


def features_body(steps, g, dpre, cw, out):
    table = conv_table(cw[0], cw[1])
    here = table[PAIR:]
    ahead = table[:PAIR]
    half = steps // 2
    for j in range(half):
        cols = slice(j * PAIR, (j + 1) * PAIR)
        total = g[:, cols].astype(F32) + dot_nt(dpre[:, 2 * j * PAIR : (2 * j + 2) * PAIR], here)
        if j + 1 < half:
            total = total + dot_nt(dpre[:, (2 * j + 2) * PAIR : (2 * j + 4) * PAIR], ahead)
        out[:, cols] = total.astype(BF16)


def hop_body(adj, own, f1, f2, f3, f4, out):
    total = dot(adj[0], own[...])
    for n, f in zip(HOP1_ORDER, (f1, f2, f3, f4)):
        total = total + dot(adj[n], f[...])
    out[...] = total.astype(BF16)


def mix_body(steps, adj, hop1, f1, f2, f3, f4, x, gated, dw, out):
    total = dot(adj[0], hop1[...])
    for n, f in zip(HOP2_ORDER, (f1, f2, f3, f4)):
        total = total + dot(adj[n], f[...])
    hop2 = total.astype(BF16)
    t0, t1, t2 = diff_table(dw[0]), diff_table(dw[1]), diff_table(dw[2])
    for j in range(steps // 2):
        cols = slice(j * PAIR, (j + 1) * PAIR)
        mixed = x[:, cols].astype(F32) + dot(gated[:, cols], t0)
        mixed = mixed + dot(hop1[:, cols], t1) + dot(hop2[:, cols], t2)
        out[:, cols] = mixed.astype(BF16)


def copies_body(parts, out):
    out[...] = jnp.broadcast_to(jnp.sum(parts[...], axis=0, keepdims=True), out.shape)


def finish_body(scale, full, diff, conv, bias):
    conv[0] = full[:CH] * scale
    conv[1] = full[CH:PAIR] * scale
    both = full[DIFF_ROWS : DIFF_ROWS + CH] * scale
    last = full[DIFF_ROWS + CH : BIAS_ROW] * scale
    diff[0] = both[:, :CH]
    diff[1] = half_turn(both)[:, :CH]
    diff[2, :32] = last[:, :CH]
    diff[2, 32:] = half_turn(last)[:, :CH]
    bias[...] = full[BIAS_ROW : BIAS_ROW + 1] * scale


def local(x, g, cw, cb, dw, tiles, source, target, count):
    cells, width = x.shape
    steps = width // CH
    devices = lax.axis_size(ALL)
    scale = 1.0 / math.sqrt(cells * devices * steps)
    field = ((cells, width), BF16)
    field32 = ((cells, width), F32)
    mac = 2 * cells * width

    (adj,) = call(
        adjacency_body,
        [((5, 2 * BLK, 2 * BLK), BF16)],
        (source, target, count, tiles),
        [SMEM, SMEM, SMEM, VMEM],
        0,
        [pltpu.VMEM((10, 2 * BLK, BLK), F32)],
    )

    *parts, own = call(
        first_body, [field] * 4 + [field32], (adj, g), [VMEM] * 2, mac * 5 * 2 * BLK
    )
    arrived = trade(parts)
    gated, dfilt, dgate, back, sums = call(
        lambda *r: gate_body(steps, *r),
        [field, field32, field32, field32, ((PAIR, PAIR), F32)],
        (x, cw, cb.reshape(1, -1), g, dw),
        [VMEM] * 5,
        mac * 2 * PAIR,
    )
    u1, *parts, own = call(
        second_body,
        [field] * 5 + [field32],
        (adj, own, *ordered(arrived, BACK1_ORDER)),
        [VMEM] * 6,
        mac * 5 * 2 * BLK,
    )
    arrived = trade(parts)
    dpre, partial = call(
        lambda *r: late_body(steps, *r),
        [((cells, 2 * width), BF16), ((ROWS, PAIR), F32)],
        (x, gated, dfilt, dgate, own, *ordered(arrived, BACK2_ORDER), back, sums, dw, u1),
        [VMEM] * 13,
        mac * 6 * PAIR,
    )
    plane, depth = ("r", "x", "c"), lax.axis_size("z")
    width_p = lax.axis_size(plane)
    rows = ROWS // width_p
    piece = lax.all_to_all(partial.reshape(width_p, rows, PAIR), plane, 0, 0, tiled=True)
    piece = jnp.broadcast_to(jnp.sum(piece, axis=0), (depth, rows, PAIR))
    piece = lax.all_to_all(piece, "z", 0, 0, tiled=True)
    (piece,) = call(copies_body, [((width_p, rows, PAIR), F32)], (piece,), [VMEM], 0)
    full = lax.all_to_all(piece, plane, 0, 0, tiled=True).reshape(ROWS, PAIR)

    (grad_features,) = call(
        lambda *r: features_body(steps, *r),
        [field],
        (g, dpre, cw),
        [VMEM] * 3,
        mac * 4 * PAIR,
    )
    (hop1,) = call(
        hop_body, [field], (adj, gated, *ordered(trade([gated] * 4), HOP1_ORDER)), [VMEM] * 6, mac * 5 * 2 * BLK
    )
    (mixed,) = call(
        lambda *r: mix_body(steps, *r),
        [field],
        (adj, hop1, *ordered(trade([hop1] * 4), HOP2_ORDER), x, gated, dw),
        [VMEM] * 9,
        mac * 8 * 2 * BLK,
    )
    diff, conv, bias = call(
        lambda *r: finish_body(scale, *r),
        [((3, CH, CH), F32), ((2, CH, PAIR), F32), ((1, PAIR), F32)],
        (full,),
        [VMEM],
        0,
    )
    return mixed, grad_features, diff, conv, bias.reshape(-1)


def solution(mesh):
    region, dom = mesh.devices.shape
    grid = mesh.devices.reshape(region, dom // 16, 8, 2)
    split = P(ALL, None)
    in_specs = (split, split, P(), P(), P(), P(ALL, None, None), split, split, P(ALL))
    out_specs = (split, split, P(), P(), P())
    return jax.shard_map(
        local,
        mesh=jax.sharding.Mesh(grid, ALL),
        in_specs=in_specs,
        out_specs=out_specs,
        check_vma=False,
    )
```
